32 devices in a mesh: grp: 2 (over y), bx: 4 (over x, core), by: 4 (over z).
Axes of the slice: x: 2, y: 2, z: 4, core: 2. Of those that a mesh axis runs over, the one named last changes fastest.
Arguments:
- volume: bfloat16 [128, 64, 128], P(('grp', 'bx'), 'by'), parts along dimension 0, may hold values from -6 to 6
- labels: int32 [64, 32, 64], P(('grp', 'bx'), 'by'), parts along dimension 0, may hold values from 0 to 15
- depth_order: int32 [8, 4], P('grp'), parts along dimension 0, may hold values from 0 to 3, as said below
- view_shear: int32 [8], P('grp'), parts along dimension 0, may hold values from -2 to 2
- tf_index: int32 [16], replicated, may hold values from 0 to 255
- color_table: float32 [256, 4], replicated, may hold values from 0.1 to 1
Outputs:
- image: float32 [8, 4, 64, 128], P(('grp', 'bx'), None, 'by'), parts along dimension 0
The draws below stay inside these ranges and needn't reach their ends.
There are 2 independent parts, one for each index of `grp`. The reference program is written for one: setup_inputs(seed, part) draws one part's arguments, and reference() takes and returns one part's arrays. A program takes and returns all parts, laid end to end along the dimension named above; an argument that names none is the same for every part. Nothing has to cross between parts.
Inputs may be any that keep to these rules, and one draw needn't show every extreme that they name: `depth_order`: each row is 0, 1, ..., 3 in ascending or in descending order.
All inputs are finite; a program needn't handle non-finite values.
Results may differ from the reference program's by a relative error of at most 0.0003.
Values may be sent and summed in bfloat16 or wider, within the bound.
A program may use at most 64 MiB of HBM per device.

```python
import jax
import jax.numpy as jnp
from jax import lax

Z = 128
CLASSES = 16
TF_ROWS = 256
X = 64
Y = 64
VIEWS = 4
N_BX = 4


def draw_depth_order(key, part):
    key = jax.random.fold_in(key, 7)
    flipped = jax.random.randint(key, (VIEWS, 1), 0, 2)
    bricks = jnp.arange(N_BX, dtype=jnp.int32)[None, :]
    return jnp.where(flipped == 1, N_BX - 1 - bricks, bricks).astype(jnp.int32)


def place_ends(entries, own_key, least, high):
    longest = entries.shape.index(max(entries.shape))
    spots = []
    for shift in (0, 1):
        where = [jax.random.randint(jax.random.fold_in(own_key, axis), (), 0, length) for axis, length in enumerate(entries.shape)]
        where[longest] = (where[longest] + shift) % entries.shape[longest]
        spots.append(tuple(where))
    return entries.at[spots[0]].set(least).at[spots[1]].set(high)


def levels(stream_key, shape, split, low, high):
    level, own = 1.0, jax.random.fold_in(stream_key, 6)
    for dim, parts in split:
        heights = jnp.exp(jax.random.uniform(jax.random.fold_in(own, dim), (parts,), jnp.float32, low / len(split), high / len(split)))
        level = level * jnp.repeat(heights, shape[dim] // parts).reshape([-1 if axis == dim else 1 for axis in range(len(shape))])
    return level


def gaussian(key, extent, scale, bound, split=(), kind=jnp.bfloat16):
    gain = levels(key, extent, split, -0.22, 0.18) if split else 1.0
    entries = jax.random.normal(key, extent, jnp.float32) * scale * gain
    return jnp.minimum(jnp.maximum(entries, -bound), bound).astype(kind)


def setup_inputs(seed: int = 0, part: int = 0) -> dict:
    key_of = jax.random.split(jax.random.key(seed), 7)
    own_keys = jax.random.split(jax.random.fold_in(key_of[6], part), 7)
    return {
        "volume": gaussian(own_keys[0], (X, Y, Z), 1.0, 6.0, ((0, 4), (1, 4))),
        "labels": place_ends(jax.random.randint(own_keys[1], (X // 2, Y // 2, Z // 2), 0, CLASSES), jax.random.fold_in(own_keys[1], 1), 0, CLASSES - 1).astype(jnp.int32),
        "depth_order": draw_depth_order(jax.random.fold_in(jax.random.fold_in(key_of[6], part), 71), part),
        "view_shear": place_ends(jax.random.randint(own_keys[3], (VIEWS,), -2, 3), jax.random.fold_in(own_keys[3], 1), -2, 2).astype(jnp.int32),
        "tf_index": place_ends(jax.random.randint(key_of[4], (CLASSES,), 0, TF_ROWS), jax.random.fold_in(key_of[4], 1), 0, TF_ROWS - 1).astype(jnp.int32),
        "color_table": jnp.clip(jax.random.uniform(key_of[5], (TF_ROWS, 4), jnp.float32, 0.1, 1.0), 0.1, 1.0),
    }


def reference(volume, labels, depth_order, view_shear, tf_index, color_table):
    class_color = color_table[tf_index]
    ascending = depth_order[:, 0] == 0
    dens_pad = jnp.pad(volume.astype(jnp.float32), ((1, 1), (0, 0), (0, 0)))
    pad_z = Z // 4
    views = depth_order.shape[0]

    def step(carry, index):
        color, depth = carry
        three = lax.dynamic_slice_in_dim(dens_pad, index, 3, 0)
        centre = three[1]
        grad_x = (three[2] - three[0]) * 0.5
        ypad = jnp.pad(centre, ((1, 1), (0, 0)))
        grad_y = (ypad[2:] - ypad[:-2]) * 0.5
        zpad = jnp.pad(centre, ((0, 0), (1, 1)))
        grad_z = (zpad[:, 2:] - zpad[:, :-2]) * 0.5
        grad_sq = grad_x * grad_x + grad_y * grad_y + grad_z * grad_z
        edge = grad_sq / (1.0 + grad_sq)
        coarse = lax.dynamic_index_in_dim(labels, index // 2, 0, keepdims=False)
        finer = jnp.repeat(jnp.repeat(coarse, 2, 0), 2, 1)
        rgbo = jnp.moveaxis(class_color[finer], -1, 0)
        tau = (6.0 / X) * jax.nn.sigmoid(2.0 * centre) * rgbo[3] * (0.25 + edge)
        alpha = -jnp.expm1(-tau)
        emission = rgbo[:3] * (0.5 + 0.5 * jnp.tanh(centre))
        field = jnp.concatenate([alpha[None] * emission, tau[None]], 0)
        field_pad = jnp.pad(field, ((0, 0), (0, 0), (pad_z, pad_z)))
        offsets = (view_shear * index * Z) // (8 * X)
        sheared = jax.vmap(lambda offset: lax.dynamic_slice_in_dim(field_pad, pad_z - offset, Z, 2))(offsets)
        slab_tau = sheared[:, 3]
        slab_col = sheared[:, :3]
        forward = color + jnp.exp(-depth)[:, None] * slab_col
        backward = slab_col + jnp.exp(-slab_tau)[:, None] * color
        color = jnp.where(ascending[:, None, None, None], forward, backward)
        depth = depth + slab_tau
        return (color, depth), None

    start = (jnp.zeros((views, 3, Y, Z), jnp.float32), jnp.zeros((views, Y, Z), jnp.float32))
    (color, depth), _ = lax.scan(step, start, jnp.arange(X, dtype=jnp.int32))
    return jnp.concatenate([color, (-jnp.expm1(-depth))[:, None]], 1)
```

```python
import functools
import math

import jax
import jax.numpy as jnp
from jax import lax
from jax.experimental import pallas as pl
from jax.experimental.pallas import tpu as pltpu
from jax.sharding import PartitionSpec as P

MESH = pl.DeviceIdType.MESH


def one_minus_exp(depth):
    series = 1.0 - depth * (1.0 / 6.0)
    for term in (5.0, 4.0, 3.0, 2.0):
        series = 1.0 - depth * (1.0 / term) * series
    return jnp.where(depth < 0.125, depth * series, 1.0 - jnp.exp(-depth))


def render(
    bricks,
    columns,
    vol_ref,
    lab_ref,
    order_ref,
    shear_ref,
    tf_ref,
    color_ref,
    out_ref,
    plane_ref,
    edge_ref,
    row_ref,
    rgbo_ref,
    field_ref,
    part_ref,
    got_ref,
    halo_send,
    halo_recv,
    part_send,
    part_recv,
):
    brick_x, brick_y, cells_z = vol_ref.shape
    half_x, half_y, half_z = lab_ref.shape
    views = order_ref.shape[0]
    per_dev = views // bricks
    x_cells = brick_x * bricks
    me = lax.axis_index("bx")
    col = lax.axis_index("by")
    has_left, has_right = me > 0, me < bricks - 1
    has_up, has_down = col > 0, col < columns - 1

    barrier = pltpu.get_barrier_semaphore()
    for step in range(1, bricks):
        other = lax.rem(me + step, bricks)
        pl.semaphore_signal(barrier, inc=1, device_id={"bx": other}, device_id_type=MESH)

    @pl.when(has_up)
    def _():
        pl.semaphore_signal(barrier, inc=1, device_id={"by": col - 1}, device_id_type=MESH)

    @pl.when(has_down)
    def _():
        pl.semaphore_signal(barrier, inc=1, device_id={"by": col + 1}, device_id_type=MESH)

    for x in range(brick_x):
        plane = vol_ref[x].astype(jnp.float32)
        edge_ref[0, x : x + 1, :] = plane[brick_y - 1 :, :]
        edge_ref[1, x : x + 1, :] = plane[:1, :]

    amount = bricks - 1 + has_up.astype(jnp.int32) + has_down.astype(jnp.int32)
    pl.semaphore_wait(barrier, amount)

    def copy(index, src, dst, target):
        return pltpu.make_async_remote_copy(
            src_ref=src,
            dst_ref=dst,
            send_sem=halo_send.at[index],
            recv_sem=halo_recv.at[index],
            device_id=target,
            device_id_type=MESH,
        )

    halos = (
        (copy(0, vol_ref.at[brick_x - 1], plane_ref.at[0], {"bx": me + 1}), has_right, has_left, plane_ref, 0),
        (copy(1, vol_ref.at[0], plane_ref.at[1], {"bx": me - 1}), has_left, has_right, plane_ref, 1),
        (copy(2, edge_ref.at[0], row_ref.at[0], {"by": col + 1}), has_down, has_up, row_ref, 0),
        (copy(3, edge_ref.at[1], row_ref.at[1], {"by": col - 1}), has_up, has_down, row_ref, 1),
    )
    for halo, sends, receives, ref, slot in halos:
        pl.when(sends)(halo.start)

        @pl.when(jnp.logical_not(receives))
        def _():
            ref[slot] = jnp.zeros(ref.shape[1:], ref.dtype)

    lane = lax.broadcasted_iota(jnp.int32, (4, 128), 1)
    row_of = jnp.zeros((4, 128), jnp.int32)
    for index in range(tf_ref.shape[0]):
        row_of = jnp.where(lane == index, tf_ref[index], row_of)
    table = jnp.zeros((4, 128), jnp.float32)
    for base in range(0, color_ref.shape[1], 128):
        local = row_of - base
        inside = jnp.logical_and(local >= 0, local < 128)
        found = jnp.take_along_axis(
            color_ref[:, base : base + 128],
            jnp.where(inside, local, 0),
            axis=1,
            mode="promise_in_bounds",
        )
        table = jnp.where(inside, found, table)
    spread = (
        lax.broadcasted_iota(jnp.int32, (half_z, cells_z), 1) // 2
        == lax.broadcasted_iota(jnp.int32, (half_z, cells_z), 0)
    ).astype(jnp.bfloat16)
    rows, fine_rows = half_x * half_y, half_x * brick_y
    repeat = (
        lax.broadcasted_iota(jnp.int32, (fine_rows, rows), 0) // 2
        == lax.broadcasted_iota(jnp.int32, (fine_rows, rows), 1)
    ).astype(jnp.bfloat16)
    coarse = lab_ref[...].reshape(rows, half_z).astype(jnp.float32).astype(jnp.bfloat16)
    wide = jnp.dot(coarse, spread, preferred_element_type=jnp.float32).astype(jnp.bfloat16)
    fine = jnp.dot(repeat, wide, preferred_element_type=jnp.float32).astype(jnp.int32)
    for chan in range(4):
        entries = jnp.broadcast_to(table[chan : chan + 1], (fine_rows, 128))
        values = jnp.take_along_axis(entries, fine, axis=1, mode="promise_in_bounds")
        for x in range(half_x):
            rgbo_ref[x, chan] = values[x * brick_y : (x + 1) * brick_y]

    for halo, sends, receives, ref, slot in halos:
        pl.when(receives)(halo.wait_recv)

    row = lax.broadcasted_iota(jnp.int32, (brick_y, cells_z), 0)
    depth_lane = lax.broadcasted_iota(jnp.int32, (brick_y, cells_z), 1)

    def dens(x):
        if x < 0:
            return plane_ref[0].astype(jnp.float32)
        if x == brick_x:
            return plane_ref[1].astype(jnp.float32)
        return vol_ref[x].astype(jnp.float32)

    for x in range(brick_x):
        centre = dens(x)
        grad_x = (dens(x + 1) - dens(x - 1)) * 0.5
        above = jnp.where(row == 0, row_ref[0, x : x + 1, :], pltpu.roll(centre, 1, 0))
        below = jnp.where(
            row == brick_y - 1, row_ref[1, x : x + 1, :], pltpu.roll(centre, brick_y - 1, 0)
        )
        grad_y = (below - above) * 0.5
        before = jnp.where(depth_lane == 0, 0.0, pltpu.roll(centre, 1, 1))
        after = jnp.where(depth_lane == cells_z - 1, 0.0, pltpu.roll(centre, cells_z - 1, 1))
        grad_z = (after - before) * 0.5
        grad_sq = grad_x * grad_x + grad_y * grad_y + grad_z * grad_z
        edge = grad_sq / (1.0 + grad_sq)
        glow = 1.0 / (1.0 + jnp.exp(-2.0 * centre))
        tau = 6.0 / x_cells * glow * rgbo_ref[x // 2, 3] * (0.25 + edge)
        gain = one_minus_exp(tau) * glow
        for chan in range(3):
            field_ref[x, chan] = gain * rgbo_ref[x // 2, chan]
        field_ref[x, 3] = tau

    shrink = math.gcd(cells_z, 8 * x_cells)
    numer, denom = cells_z // shrink, 8 * x_cells // shrink

    def send_of(view):
        owner = lax.div(view, per_dev)
        local = lax.rem(view, per_dev)
        return owner, local, pltpu.make_async_remote_copy(
            src_ref=part_ref.at[view],
            dst_ref=got_ref.at[me, local],
            send_sem=part_send.at[view],
            recv_sem=part_recv.at[me, local],
            device_id={"bx": owner},
            device_id_type=MESH,
        )

    def one_view(step, carry):
        view = lax.rem((me + 1) * per_dev + step, views)
        ascending = order_ref[view, 0] == 0
        shear = shear_ref[view]
        color = [jnp.zeros((brick_y, cells_z), jnp.float32) for _ in range(3)]
        depth = jnp.zeros((brick_y, cells_z), jnp.float32)
        for index in range(brick_x):
            x = jnp.where(ascending, index, brick_x - 1 - index)
            scaled = shear * (me * brick_x + x) * numer
            ahead = lax.div(scaled + denom * cells_z, denom)
            turn = lax.rem(ahead, cells_z)
            source = depth_lane + (cells_z - ahead)
            inside = jnp.logical_and(source >= 0, source < cells_z)
            moved = pltpu.roll(field_ref[x].reshape(4 * brick_y, cells_z), turn, 1)
            seen = jnp.where(inside, jnp.exp(-depth), 0.0)
            for chan in range(3):
                color[chan] = color[chan] + seen * moved[chan * brick_y : (chan + 1) * brick_y]
            depth = depth + jnp.where(inside, moved[3 * brick_y :], 0.0)
        owner, local, send = send_of(view)

        @pl.when(owner != me)
        def _():
            for chan in range(3):
                part_ref[view, chan] = color[chan]
            part_ref[view, 3] = depth
            send.start()

        @pl.when(owner == me)
        def _():
            for chan in range(3):
                got_ref[me, local, chan] = color[chan]
            got_ref[me, local, 3] = depth

        return carry

    lax.fori_loop(0, views, one_view, 0)

    for step in range(1, bricks):
        source = lax.rem(me + step, bricks)
        for local in range(per_dev):
            pltpu.make_async_remote_copy(
                src_ref=part_ref.at[0],
                dst_ref=got_ref.at[source, local],
                send_sem=part_send.at[0],
                recv_sem=part_recv.at[source, local],
                device_id={"bx": source},
                device_id_type=MESH,
            ).wait_recv()

    for local in range(per_dev):
        ascending = order_ref[me * per_dev + local, 0] == 0
        color = [jnp.zeros((brick_y, cells_z), jnp.float32) for _ in range(3)]
        depth = jnp.zeros((brick_y, cells_z), jnp.float32)
        for index in range(bricks):
            brick = jnp.where(ascending, index, bricks - 1 - index)
            seen = jnp.exp(-depth)
            for chan in range(3):
                color[chan] = color[chan] + seen * got_ref[brick, local, chan]
            depth = depth + got_ref[brick, local, 3]
        for chan in range(3):
            out_ref[local, chan] = color[chan]
        out_ref[local, 3] = one_minus_exp(depth)

    for halo, sends, receives, ref, slot in halos:
        pl.when(sends)(halo.wait_send)
    for step in range(views - per_dev):
        view = lax.rem((me + 1) * per_dev + step, views)
        send_of(view)[2].wait_send()


def on_device(bricks, columns, volume, labels, depth_order, view_shear, tf_index, color_table):
    brick_x, brick_y, cells_z = volume.shape
    views = depth_order.shape[0]
    per_dev = views // bricks
    image = (4, brick_y, cells_z)
    vmem = pl.BlockSpec(memory_space=pltpu.VMEM)
    smem = pl.BlockSpec(memory_space=pltpu.SMEM)
    return pl.pallas_call(
        functools.partial(render, bricks, columns),
        out_shape=jax.ShapeDtypeStruct((per_dev,) + image, jnp.float32),
        in_specs=[vmem, vmem, smem, smem, smem, vmem],
        out_specs=vmem,
        scratch_shapes=[
            pltpu.VMEM((2, brick_y, cells_z), volume.dtype),
            pltpu.VMEM((2, brick_x, cells_z), jnp.float32),
            pltpu.VMEM((2, brick_x, cells_z), jnp.float32),
            pltpu.VMEM((labels.shape[0],) + image, jnp.float32),
            pltpu.VMEM((brick_x,) + image, jnp.float32),
            pltpu.VMEM((views,) + image, jnp.float32),
            pltpu.VMEM((bricks, per_dev) + image, jnp.float32),
            pltpu.SemaphoreType.DMA((4,)),
            pltpu.SemaphoreType.DMA((4,)),
            pltpu.SemaphoreType.DMA((views,)),
            pltpu.SemaphoreType.DMA((bricks, per_dev)),
        ],
        compiler_params=pltpu.CompilerParams(
            collective_id=0, has_side_effects=True, vmem_limit_bytes=32 * 2**20
        ),
    )(volume, labels, depth_order, view_shear, tf_index, color_table.T)


def solution(mesh):
    return jax.shard_map(
        functools.partial(on_device, mesh.shape["bx"], mesh.shape["by"]),
        mesh=mesh,
        in_specs=(
            P(("grp", "bx"), "by", None),
            P(("grp", "bx"), "by", None),
            P("grp", None),
            P("grp"),
            P(),
            P(),
        ),
        out_specs=P(("grp", "bx"), None, "by", None),
        check_vma=False,
    )
```

```python
import functools
import math

import jax
import jax.numpy as jnp
from jax import lax
from jax.experimental import pallas as pl
from jax.experimental.pallas import tpu as pltpu
from jax.sharding import PartitionSpec as P

MESH = pl.DeviceIdType.MESH


def one_minus_exp(depth):
    series = 1.0 - depth * (1.0 / 6.0)
    for term in (5.0, 4.0, 3.0, 2.0):
        series = 1.0 - depth * (1.0 / term) * series
    return jnp.where(depth < 0.125, depth * series, 1.0 - jnp.exp(-depth))


def render(
    bricks,
    columns,
    vol_hbm,
    lab_hbm,
    order_hbm,
    shear_hbm,
    tf_hbm,
    color_hbm,
    out_ref,
    vol_ref,
    lab_ref,
    order_ref,
    shear_ref,
    tf_ref,
    color_ref,
    glow_ref,
    grad_ref,
    plane_ref,
    edge_ref,
    row_ref,
    rgbo_ref,
    field_ref,
    part_ref,
    got_ref,
    halo_send,
    halo_recv,
    part_send,
    part_recv,
    load_sem,
):
    brick_x, brick_y, cells_z = vol_ref.shape
    half_x, half_y, half_z = lab_ref.shape
    views = order_ref.shape[0]
    per_dev = views // bricks
    x_cells = brick_x * bricks
    me = lax.axis_index("bx")
    col = lax.axis_index("by")
    has_left, has_right = me > 0, me < bricks - 1
    has_up, has_down = col > 0, col < columns - 1

    barrier = pltpu.get_barrier_semaphore()
    for step in range(1, bricks):
        other = lax.rem(me + step, bricks)
        pl.semaphore_signal(barrier, inc=1, device_id={"bx": other}, device_id_type=MESH)

    @pl.when(has_up)
    def _():
        pl.semaphore_signal(barrier, inc=1, device_id={"by": col - 1}, device_id_type=MESH)

    @pl.when(has_down)
    def _():
        pl.semaphore_signal(barrier, inc=1, device_id={"by": col + 1}, device_id_type=MESH)

    pairs = (
        (vol_hbm, vol_ref),
        (lab_hbm, lab_ref),
        (tf_hbm, tf_ref),
        (color_hbm, color_ref),
        (order_hbm, order_ref),
        (shear_hbm, shear_ref),
    )
    loads = [
        pltpu.make_async_copy(source, target, load_sem.at[index])
        for index, (source, target) in enumerate(pairs)
    ]
    for load in loads:
        load.start()
    loads[0].wait()

    for x in range(brick_x):
        plane = vol_ref[x].astype(jnp.float32)
        edge_ref[0, x : x + 1, :] = plane[brick_y - 1 :, :]
        edge_ref[1, x : x + 1, :] = plane[:1, :]

    amount = bricks - 1 + has_up.astype(jnp.int32) + has_down.astype(jnp.int32)
    pl.semaphore_wait(barrier, amount)

    def copy(index, src, dst, target):
        return pltpu.make_async_remote_copy(
            src_ref=src,
            dst_ref=dst,
            send_sem=halo_send.at[index],
            recv_sem=halo_recv.at[index],
            device_id=target,
            device_id_type=MESH,
        )

    halos = (
        (copy(0, vol_ref.at[brick_x - 1], plane_ref.at[0], {"bx": me + 1}), has_right, has_left, plane_ref, 0),
        (copy(1, vol_ref.at[0], plane_ref.at[1], {"bx": me - 1}), has_left, has_right, plane_ref, 1),
        (copy(2, edge_ref.at[0], row_ref.at[0], {"by": col + 1}), has_down, has_up, row_ref, 0),
        (copy(3, edge_ref.at[1], row_ref.at[1], {"by": col - 1}), has_up, has_down, row_ref, 1),
    )
    for halo, sends, receives, ref, slot in halos:
        pl.when(sends)(halo.start)

        @pl.when(jnp.logical_not(receives))
        def _():
            ref[slot] = jnp.zeros(ref.shape[1:], ref.dtype)

    for load in loads[1:]:
        load.wait()

    lane = lax.broadcasted_iota(jnp.int32, (4, 128), 1)
    row_of = jnp.zeros((4, 128), jnp.int32)
    for index in range(tf_ref.shape[0]):
        row_of = jnp.where(lane == index, tf_ref[index], row_of)
    table = jnp.zeros((4, 128), jnp.float32)
    for base in range(0, color_ref.shape[1], 128):
        local = row_of - base
        inside = jnp.logical_and(local >= 0, local < 128)
        found = jnp.take_along_axis(
            color_ref[:, base : base + 128],
            jnp.where(inside, local, 0),
            axis=1,
            mode="promise_in_bounds",
        )
        table = jnp.where(inside, found, table)
    spread = (
        lax.broadcasted_iota(jnp.int32, (half_z, cells_z), 1) // 2
        == lax.broadcasted_iota(jnp.int32, (half_z, cells_z), 0)
    ).astype(jnp.bfloat16)
    rows, fine_rows = half_x * half_y, half_x * brick_y
    repeat = (
        lax.broadcasted_iota(jnp.int32, (fine_rows, rows), 0) // 2
        == lax.broadcasted_iota(jnp.int32, (fine_rows, rows), 1)
    ).astype(jnp.bfloat16)
    coarse = lab_ref[...].reshape(rows, half_z).astype(jnp.float32).astype(jnp.bfloat16)
    wide = jnp.dot(coarse, spread, preferred_element_type=jnp.float32).astype(jnp.bfloat16)
    fine = jnp.dot(repeat, wide, preferred_element_type=jnp.float32).astype(jnp.int32)
    for chan in range(4):
        entries = jnp.broadcast_to(table[chan : chan + 1], (fine_rows, 128))
        values = jnp.take_along_axis(entries, fine, axis=1, mode="promise_in_bounds")
        for x in range(half_x):
            rgbo_ref[x, chan] = values[x * brick_y : (x + 1) * brick_y]

    row = lax.broadcasted_iota(jnp.int32, (brick_y, cells_z), 0)
    depth_lane = lax.broadcasted_iota(jnp.int32, (brick_y, cells_z), 1)

    def dens(x):
        if x < 0:
            return plane_ref[0].astype(jnp.float32)
        if x == brick_x:
            return plane_ref[1].astype(jnp.float32)
        return vol_ref[x].astype(jnp.float32)

    for x in range(brick_x):
        centre = dens(x)
        before = jnp.where(depth_lane == 0, 0.0, pltpu.roll(centre, 1, 1))
        after = jnp.where(depth_lane == cells_z - 1, 0.0, pltpu.roll(centre, cells_z - 1, 1))
        grad_z = (after - before) * 0.5
        grad_sq = grad_z * grad_z
        if 0 < x < brick_x - 1:
            grad_x = (dens(x + 1) - dens(x - 1)) * 0.5
            grad_sq = grad_sq + grad_x * grad_x
        grad_ref[x] = grad_sq
        glow_ref[x] = 1.0 / (1.0 + jnp.exp(-2.0 * centre))

    for halo, sends, receives, ref, slot in halos:
        pl.when(receives)(halo.wait_recv)

    for x in range(brick_x):
        centre = dens(x)
        grad_sq = grad_ref[x]
        if x == 0 or x == brick_x - 1:
            grad_x = (dens(x + 1) - dens(x - 1)) * 0.5
            grad_sq = grad_sq + grad_x * grad_x
        above = jnp.where(row == 0, row_ref[0, x : x + 1, :], pltpu.roll(centre, 1, 0))
        below = jnp.where(
            row == brick_y - 1, row_ref[1, x : x + 1, :], pltpu.roll(centre, brick_y - 1, 0)
        )
        grad_y = (below - above) * 0.5
        grad_sq = grad_sq + grad_y * grad_y
        edge = grad_sq / (1.0 + grad_sq)
        glow = glow_ref[x]
        tau = 6.0 / x_cells * glow * rgbo_ref[x // 2, 3] * (0.25 + edge)
        gain = one_minus_exp(tau) * glow
        for chan in range(3):
            field_ref[x, chan] = gain * rgbo_ref[x // 2, chan]
        field_ref[x, 3] = tau

    shrink = math.gcd(cells_z, 8 * x_cells)
    numer, denom = cells_z // shrink, 8 * x_cells // shrink

    def ahead_of(scaled):
        if denom & (denom - 1) == 0:
            return lax.shift_right_arithmetic(scaled, denom.bit_length() - 1) + cells_z
        return lax.div(scaled + denom * cells_z, denom)

    def composite(view):
        ascending = order_ref[view, 0] == 0
        shear = shear_ref[view]
        color = [jnp.zeros((brick_y, cells_z), jnp.float32) for _ in range(3)]
        depth = jnp.zeros((brick_y, cells_z), jnp.float32)
        for index in range(brick_x):
            x = jnp.where(ascending, index, brick_x - 1 - index)
            ahead = ahead_of(shear * (me * brick_x + x) * numer)
            turn = jnp.where(ahead >= cells_z, ahead - cells_z, ahead)
            source = depth_lane + (cells_z - ahead)
            inside = jnp.logical_and(source >= 0, source < cells_z)
            moved = pltpu.roll(field_ref[x].reshape(4 * brick_y, cells_z), turn, 1)
            seen = jnp.where(inside, jnp.exp(-depth), 0.0)
            for chan in range(3):
                color[chan] = color[chan] + seen * moved[chan * brick_y : (chan + 1) * brick_y]
            depth = depth + jnp.where(inside, moved[3 * brick_y :], 0.0)
        return color + [depth]

    def send_of(view):
        owner = lax.div(view, per_dev)
        local = lax.rem(view, per_dev)
        return pltpu.make_async_remote_copy(
            src_ref=part_ref.at[view],
            dst_ref=got_ref.at[me, local],
            send_sem=part_send.at[view],
            recv_sem=part_recv.at[me, local],
            device_id={"bx": owner},
            device_id_type=MESH,
        )

    def other_view(step):
        view = lax.rem((me + 1) * per_dev + step, views)
        for chan, values in enumerate(composite(view)):
            part_ref[view, chan] = values
        send_of(view).start()

    if views <= 4:
        for step in range(views - per_dev):
            other_view(step)
    else:
        pl.loop(0, views - per_dev)(other_view)
    for local in range(per_dev):
        for chan, values in enumerate(composite(me * per_dev + local)):
            got_ref[me, local, chan] = values

    for step in range(1, bricks):
        source = lax.rem(me + step, bricks)
        for local in range(per_dev):
            pltpu.make_async_remote_copy(
                src_ref=part_ref.at[0],
                dst_ref=got_ref.at[source, local],
                send_sem=part_send.at[0],
                recv_sem=part_recv.at[source, local],
                device_id={"bx": source},
                device_id_type=MESH,
            ).wait_recv()

    for local in range(per_dev):
        ascending = order_ref[me * per_dev + local, 0] == 0
        color = [jnp.zeros((brick_y, cells_z), jnp.float32) for _ in range(3)]
        depth = jnp.zeros((brick_y, cells_z), jnp.float32)
        for index in range(bricks):
            brick = jnp.where(ascending, index, bricks - 1 - index)
            seen = jnp.exp(-depth)
            for chan in range(3):
                color[chan] = color[chan] + seen * got_ref[brick, local, chan]
            depth = depth + got_ref[brick, local, 3]
        for chan in range(3):
            out_ref[local, chan] = color[chan]
        out_ref[local, 3] = one_minus_exp(depth)

    for halo, sends, receives, ref, slot in halos:
        pl.when(sends)(halo.wait_send)
    for step in range(views - per_dev):
        view = lax.rem((me + 1) * per_dev + step, views)
        send_of(view).wait_send()


def on_device(bricks, columns, volume, labels, depth_order, view_shear, tf_index, color_table):
    brick_x, brick_y, cells_z = volume.shape
    views = depth_order.shape[0]
    per_dev = views // bricks
    image = (4, brick_y, cells_z)
    hbm = pl.BlockSpec(memory_space=pltpu.HBM)
    colors = color_table.T
    return pl.pallas_call(
        functools.partial(render, bricks, columns),
        out_shape=jax.ShapeDtypeStruct((per_dev,) + image, jnp.float32),
        in_specs=[hbm] * 6,
        out_specs=pl.BlockSpec(memory_space=pltpu.VMEM),
        scratch_shapes=[
            pltpu.VMEM(volume.shape, volume.dtype),
            pltpu.VMEM(labels.shape, labels.dtype),
            pltpu.SMEM(depth_order.shape, depth_order.dtype),
            pltpu.SMEM(view_shear.shape, view_shear.dtype),
            pltpu.SMEM(tf_index.shape, tf_index.dtype),
            pltpu.VMEM(colors.shape, colors.dtype),
            pltpu.VMEM(volume.shape, jnp.float32),
            pltpu.VMEM(volume.shape, jnp.float32),
            pltpu.VMEM((2, brick_y, cells_z), volume.dtype),
            pltpu.VMEM((2, brick_x, cells_z), jnp.float32),
            pltpu.VMEM((2, brick_x, cells_z), jnp.float32),
            pltpu.VMEM((labels.shape[0],) + image, jnp.float32),
            pltpu.VMEM((brick_x,) + image, jnp.float32),
            pltpu.VMEM((views,) + image, jnp.float32),
            pltpu.VMEM((bricks, per_dev) + image, jnp.float32),
            pltpu.SemaphoreType.DMA((4,)),
            pltpu.SemaphoreType.DMA((4,)),
            pltpu.SemaphoreType.DMA((views,)),
            pltpu.SemaphoreType.DMA((bricks, per_dev)),
            pltpu.SemaphoreType.DMA((6,)),
        ],
        compiler_params=pltpu.CompilerParams(
            collective_id=0, has_side_effects=True
        ),
    )(volume, labels, depth_order, view_shear, tf_index, colors)


def solution(mesh):
    return jax.shard_map(
        functools.partial(on_device, mesh.shape["bx"], mesh.shape["by"]),
        mesh=mesh,
        in_specs=(
            P(("grp", "bx"), "by", None),
            P(("grp", "bx"), "by", None),
            P("grp", None),
            P("grp"),
            P(),
            P(),
        ),
        out_specs=P(("grp", "bx"), None, "by", None),
        check_vma=False,
    )
```

```python
import functools
import math

import jax
import jax.numpy as jnp
from jax import lax
from jax.experimental import pallas as pl
from jax.experimental.pallas import tpu as pltpu
from jax.sharding import PartitionSpec as P

MESH = pl.DeviceIdType.MESH


def one_minus_exp(depth):
    series = 1.0 - depth * (1.0 / 6.0)
    for term in (5.0, 4.0, 3.0, 2.0):
        series = 1.0 - depth * (1.0 / term) * series
    return jnp.where(depth < 0.125, depth * series, 1.0 - jnp.exp(-depth))


def render(
    bricks,
    columns,
    vol_hbm,
    lab_hbm,
    order_hbm,
    shear_hbm,
    tf_hbm,
    color_hbm,
    out_ref,
    vol_ref,
    lab_ref,
    order_ref,
    shear_ref,
    tf_ref,
    color_ref,
    glow_ref,
    grad_ref,
    plane_ref,
    edge_ref,
    row_ref,
    rgbo_ref,
    field_ref,
    part_ref,
    got_ref,
    halo_send,
    halo_recv,
    part_send,
    part_recv,
    load_sem,
):
    brick_x, brick_y, cells_z = vol_ref.shape
    half_x, half_y, half_z = lab_ref.shape
    views = order_ref.shape[0]
    per_dev = views // bricks
    x_cells = brick_x * bricks
    me = lax.axis_index("bx")
    col = lax.axis_index("by")
    has_left, has_right = me > 0, me < bricks - 1
    has_up, has_down = col > 0, col < columns - 1

    barrier = pltpu.get_barrier_semaphore()
    for step in range(1, bricks):
        other = lax.rem(me + step, bricks)
        pl.semaphore_signal(barrier, inc=1, device_id={"bx": other}, device_id_type=MESH)

    @pl.when(has_up)
    def _():
        pl.semaphore_signal(barrier, inc=1, device_id={"by": col - 1}, device_id_type=MESH)

    @pl.when(has_down)
    def _():
        pl.semaphore_signal(barrier, inc=1, device_id={"by": col + 1}, device_id_type=MESH)

    pairs = (
        (vol_hbm, vol_ref),
        (lab_hbm, lab_ref),
        (tf_hbm, tf_ref),
        (color_hbm, color_ref),
        (order_hbm, order_ref),
        (shear_hbm, shear_ref),
    )
    loads = [
        pltpu.make_async_copy(source, target, load_sem.at[index])
        for index, (source, target) in enumerate(pairs)
    ]
    for load in loads:
        load.start()
    amount = bricks - 1 + has_up.astype(jnp.int32) + has_down.astype(jnp.int32)
    pl.semaphore_wait(barrier, amount)

    def copy(index, src, dst, target):
        return pltpu.make_async_remote_copy(
            src_ref=src,
            dst_ref=dst,
            send_sem=halo_send.at[index],
            recv_sem=halo_recv.at[index],
            device_id=target,
            device_id_type=MESH,
        )

    halos = (
        (copy(0, vol_hbm.at[brick_x - 1], plane_ref.at[0], {"bx": me + 1}), has_right, has_left, plane_ref, 0),
        (copy(1, vol_hbm.at[0], plane_ref.at[1], {"bx": me - 1}), has_left, has_right, plane_ref, 1),
        (copy(2, edge_ref.at[0], row_ref.at[0], {"by": col + 1}), has_down, has_up, row_ref, 0),
        (copy(3, edge_ref.at[1], row_ref.at[1], {"by": col - 1}), has_up, has_down, row_ref, 1),
    )
    for halo, sends, receives, ref, slot in halos[:2]:
        pl.when(sends)(halo.start)
    loads[0].wait()
    for x in range(brick_x):
        plane = vol_ref[x].astype(jnp.float32)
        edge_ref[0, x : x + 1, :] = plane[brick_y - 1 :, :]
        edge_ref[1, x : x + 1, :] = plane[:1, :]
    for halo, sends, receives, ref, slot in halos[2:]:
        pl.when(sends)(halo.start)

    for halo, sends, receives, ref, slot in halos:

        @pl.when(jnp.logical_not(receives))
        def _():
            ref[slot] = jnp.zeros(ref.shape[1:], ref.dtype)

    for load in loads[1:]:
        load.wait()

    lane = lax.broadcasted_iota(jnp.int32, (4, 128), 1)
    row_of = jnp.zeros((4, 128), jnp.int32)
    for index in range(tf_ref.shape[0]):
        row_of = jnp.where(lane == index, tf_ref[index], row_of)
    table = jnp.zeros((4, 128), jnp.float32)
    for base in range(0, color_ref.shape[1], 128):
        local = row_of - base
        inside = jnp.logical_and(local >= 0, local < 128)
        found = jnp.take_along_axis(
            color_ref[:, base : base + 128],
            jnp.where(inside, local, 0),
            axis=1,
            mode="promise_in_bounds",
        )
        table = jnp.where(inside, found, table)
    spread = (
        lax.broadcasted_iota(jnp.int32, (half_z, cells_z), 1) // 2
        == lax.broadcasted_iota(jnp.int32, (half_z, cells_z), 0)
    ).astype(jnp.bfloat16)
    rows, fine_rows = half_x * half_y, half_x * brick_y
    repeat = (
        lax.broadcasted_iota(jnp.int32, (fine_rows, rows), 0) // 2
        == lax.broadcasted_iota(jnp.int32, (fine_rows, rows), 1)
    ).astype(jnp.bfloat16)
    coarse = lab_ref[...].reshape(rows, half_z).astype(jnp.float32).astype(jnp.bfloat16)
    wide = jnp.dot(coarse, spread, preferred_element_type=jnp.float32).astype(jnp.bfloat16)
    fine = jnp.dot(repeat, wide, preferred_element_type=jnp.float32).astype(jnp.int32)
    for chan in range(4):
        entries = jnp.broadcast_to(table[chan : chan + 1], (fine_rows, 128))
        values = jnp.take_along_axis(entries, fine, axis=1, mode="promise_in_bounds")
        for x in range(half_x):
            rgbo_ref[x, chan] = values[x * brick_y : (x + 1) * brick_y]

    row = lax.broadcasted_iota(jnp.int32, (brick_y, cells_z), 0)
    depth_lane = lax.broadcasted_iota(jnp.int32, (brick_y, cells_z), 1)

    def dens(x):
        if x < 0:
            return plane_ref[0].astype(jnp.float32)
        if x == brick_x:
            return plane_ref[1].astype(jnp.float32)
        return vol_ref[x].astype(jnp.float32)

    for x in range(brick_x):
        centre = dens(x)
        before = jnp.where(depth_lane == 0, 0.0, pltpu.roll(centre, 1, 1))
        after = jnp.where(depth_lane == cells_z - 1, 0.0, pltpu.roll(centre, cells_z - 1, 1))
        grad_z = (after - before) * 0.5
        grad_sq = grad_z * grad_z
        if 0 < x < brick_x - 1:
            grad_x = (dens(x + 1) - dens(x - 1)) * 0.5
            grad_sq = grad_sq + grad_x * grad_x
        grad_ref[x] = grad_sq
        glow_ref[x] = 1.0 / (1.0 + jnp.exp(-2.0 * centre))

    for halo, sends, receives, ref, slot in halos:
        pl.when(receives)(halo.wait_recv)

    for x in range(brick_x):
        centre = dens(x)
        grad_sq = grad_ref[x]
        if x == 0 or x == brick_x - 1:
            grad_x = (dens(x + 1) - dens(x - 1)) * 0.5
            grad_sq = grad_sq + grad_x * grad_x
        above = jnp.where(row == 0, row_ref[0, x : x + 1, :], pltpu.roll(centre, 1, 0))
        below = jnp.where(
            row == brick_y - 1, row_ref[1, x : x + 1, :], pltpu.roll(centre, brick_y - 1, 0)
        )
        grad_y = (below - above) * 0.5
        grad_sq = grad_sq + grad_y * grad_y
        edge = grad_sq / (1.0 + grad_sq)
        glow = glow_ref[x]
        tau = 6.0 / x_cells * glow * rgbo_ref[x // 2, 3] * (0.25 + edge)
        gain = one_minus_exp(tau) * glow
        for chan in range(3):
            field_ref[x, chan] = gain * rgbo_ref[x // 2, chan]
        field_ref[x, 3] = tau

    shrink = math.gcd(cells_z, 8 * x_cells)
    numer, denom = cells_z // shrink, 8 * x_cells // shrink

    def ahead_of(scaled):
        if denom & (denom - 1) == 0:
            return lax.shift_right_arithmetic(scaled, denom.bit_length() - 1) + cells_z
        return lax.div(scaled + denom * cells_z, denom)

    def composite(view):
        ascending = order_ref[view, 0] == 0
        shear = shear_ref[view]
        color = [jnp.zeros((brick_y, cells_z), jnp.float32) for _ in range(3)]
        depth = jnp.zeros((brick_y, cells_z), jnp.float32)
        for index in range(brick_x):
            x = jnp.where(ascending, index, brick_x - 1 - index)
            ahead = ahead_of(shear * (me * brick_x + x) * numer)
            turn = jnp.where(ahead >= cells_z, ahead - cells_z, ahead)
            source = depth_lane + (cells_z - ahead)
            inside = jnp.logical_and(source >= 0, source < cells_z)
            moved = pltpu.roll(field_ref[x].reshape(4 * brick_y, cells_z), turn, 1)
            seen = jnp.where(inside, jnp.exp(-depth), 0.0)
            for chan in range(3):
                color[chan] = color[chan] + seen * moved[chan * brick_y : (chan + 1) * brick_y]
            depth = depth + jnp.where(inside, moved[3 * brick_y :], 0.0)
        return color + [depth]

    def send_of(view):
        owner = lax.div(view, per_dev)
        local = lax.rem(view, per_dev)
        return pltpu.make_async_remote_copy(
            src_ref=part_ref.at[view],
            dst_ref=got_ref.at[me, local],
            send_sem=part_send.at[view],
            recv_sem=part_recv.at[me, local],
            device_id={"bx": owner},
            device_id_type=MESH,
        )

    def view_at(step):
        turn = lax.div(step, per_dev)
        local = lax.rem(step, per_dev)
        pair, core = lax.div(me, 2), lax.rem(me, 2)
        pair = lax.rem(pair + 1 + lax.div(turn, 2), bricks // 2)
        core = jnp.where(turn == bricks - 2, 1 - core, lax.rem(core + turn, 2))
        return (2 * pair + core) * per_dev + local

    def other_view(step):
        view = view_at(step)
        for chan, values in enumerate(composite(view)):
            part_ref[view, chan] = values
        send_of(view).start()

    if views <= 4:
        for step in range(views - per_dev):
            other_view(jnp.int32(step))
    else:
        pl.loop(0, views - per_dev)(other_view)
    for local in range(per_dev):
        for chan, values in enumerate(composite(me * per_dev + local)):
            got_ref[me, local, chan] = values

    for step in range(1, bricks):
        source = lax.rem(me + step, bricks)
        for local in range(per_dev):
            pltpu.make_async_remote_copy(
                src_ref=part_ref.at[0],
                dst_ref=got_ref.at[source, local],
                send_sem=part_send.at[0],
                recv_sem=part_recv.at[source, local],
                device_id={"bx": source},
                device_id_type=MESH,
            ).wait_recv()

    for local in range(per_dev):
        ascending = order_ref[me * per_dev + local, 0] == 0
        color = [jnp.zeros((brick_y, cells_z), jnp.float32) for _ in range(3)]
        depth = jnp.zeros((brick_y, cells_z), jnp.float32)
        for index in range(bricks):
            brick = jnp.where(ascending, index, bricks - 1 - index)
            seen = jnp.exp(-depth)
            for chan in range(3):
                color[chan] = color[chan] + seen * got_ref[brick, local, chan]
            depth = depth + got_ref[brick, local, 3]
        for chan in range(3):
            out_ref[local, chan] = color[chan]
        out_ref[local, 3] = one_minus_exp(depth)

    for halo, sends, receives, ref, slot in halos:
        pl.when(sends)(halo.wait_send)
    for step in range(views - per_dev):
        send_of(view_at(jnp.int32(step))).wait_send()


def on_device(bricks, columns, volume, labels, depth_order, view_shear, tf_index, color_table):
    brick_x, brick_y, cells_z = volume.shape
    views = depth_order.shape[0]
    per_dev = views // bricks
    image = (4, brick_y, cells_z)
    hbm = pl.BlockSpec(memory_space=pltpu.HBM)
    colors = color_table.T
    arrays = [
        pltpu.with_memory_space_constraint(array, pltpu.HBM)
        for array in (volume, labels, depth_order, view_shear, tf_index, colors)
    ]
    return pl.pallas_call(
        functools.partial(render, bricks, columns),
        out_shape=jax.ShapeDtypeStruct((per_dev,) + image, jnp.float32),
        in_specs=[hbm] * 6,
        out_specs=pl.BlockSpec(memory_space=pltpu.VMEM),
        scratch_shapes=[
            pltpu.VMEM(volume.shape, volume.dtype),
            pltpu.VMEM(labels.shape, labels.dtype),
            pltpu.SMEM(depth_order.shape, depth_order.dtype),
            pltpu.SMEM(view_shear.shape, view_shear.dtype),
            pltpu.SMEM(tf_index.shape, tf_index.dtype),
            pltpu.VMEM(colors.shape, colors.dtype),
            pltpu.VMEM(volume.shape, jnp.float32),
            pltpu.VMEM(volume.shape, jnp.float32),
            pltpu.VMEM((2, brick_y, cells_z), volume.dtype),
            pltpu.VMEM((2, brick_x, cells_z), jnp.float32),
            pltpu.VMEM((2, brick_x, cells_z), jnp.float32),
            pltpu.VMEM((labels.shape[0],) + image, jnp.float32),
            pltpu.VMEM((brick_x,) + image, jnp.float32),
            pltpu.VMEM((views,) + image, jnp.float32),
            pltpu.VMEM((bricks, per_dev) + image, jnp.float32),
            pltpu.SemaphoreType.DMA((4,)),
            pltpu.SemaphoreType.DMA((4,)),
            pltpu.SemaphoreType.DMA((views,)),
            pltpu.SemaphoreType.DMA((bricks, per_dev)),
            pltpu.SemaphoreType.DMA((6,)),
        ],
        compiler_params=pltpu.CompilerParams(
            collective_id=0, has_side_effects=True, vmem_limit_bytes=32 * 2**20
        ),
    )(*arrays)


def solution(mesh):
    return jax.shard_map(
        functools.partial(on_device, mesh.shape["bx"], mesh.shape["by"]),
        mesh=mesh,
        in_specs=(
            P(("grp", "bx"), "by", None),
            P(("grp", "bx"), "by", None),
            P("grp", None),
            P("grp"),
            P(),
            P(),
        ),
        out_specs=P(("grp", "bx"), None, "by", None),
        check_vma=False,
    )
```

```python
import functools
import math

import jax
import jax.numpy as jnp
from jax import lax
from jax.experimental import pallas as pl
from jax.experimental.pallas import tpu as pltpu
from jax.sharding import PartitionSpec as P

MESH = pl.DeviceIdType.MESH


def one_minus_exp(depth):
    series = 1.0 - depth * (1.0 / 6.0)
    for term in (5.0, 4.0, 3.0, 2.0):
        series = 1.0 - depth * (1.0 / term) * series
    return jnp.where(depth < 0.125, depth * series, 1.0 - jnp.exp(-depth))


def render(
    bricks,
    columns,
    vol_hbm,
    lab_hbm,
    order_hbm,
    shear_hbm,
    tf_hbm,
    color_hbm,
    out_ref,
    vol_ref,
    lab_ref,
    order_ref,
    shear_ref,
    tf_ref,
    color_ref,
    glow_ref,
    grad_ref,
    plane_ref,
    edge_ref,
    row_ref,
    rgbo_ref,
    field_ref,
    part_ref,
    got_ref,
    halo_send,
    halo_recv,
    part_send,
    part_recv,
    load_sem,
    ready_sem,
):
    brick_x, brick_y, cells_z = vol_ref.shape
    half_x, half_y, half_z = lab_ref.shape
    views = order_ref.shape[0]
    per_dev = views // bricks
    x_cells = brick_x * bricks
    me = lax.axis_index("bx")
    col = lax.axis_index("by")
    has_left, has_right = me > 0, me < bricks - 1
    has_up, has_down = col > 0, col < columns - 1

    barrier = pltpu.get_barrier_semaphore()
    for step in range(1, bricks):
        other = lax.rem(me + step, bricks)
        pl.semaphore_signal(barrier, inc=1, device_id={"bx": other}, device_id_type=MESH)

    @pl.when(has_down)
    def _():
        pl.semaphore_signal(barrier, inc=1, device_id={"by": col + 1}, device_id_type=MESH)

    pairs = (
        (vol_hbm, vol_ref),
        (lab_hbm, lab_ref),
        (tf_hbm, tf_ref),
        (color_hbm, color_ref),
        (order_hbm, order_ref),
        (shear_hbm, shear_ref),
    )
    loads = [
        pltpu.make_async_copy(source, target, load_sem.at[index])
        for index, (source, target) in enumerate(pairs)
    ]
    for load in loads:
        load.start()
    loads[0].wait()
    for x in range(brick_x):
        plane = vol_ref[x].astype(jnp.float32)
        edge_ref[0, x : x + 1, :] = plane[brick_y - 1 :, :]
        edge_ref[1, x : x + 1, :] = plane[:1, :]

    amount = bricks - 1 + has_up.astype(jnp.int32)
    pl.semaphore_wait(barrier, amount)

    @pl.when(has_up)
    def _():
        pl.semaphore_signal(ready_sem, inc=1, device_id={"by": col - 1}, device_id_type=MESH)

    def copy(index, src, dst, target):
        return pltpu.make_async_remote_copy(
            src_ref=src,
            dst_ref=dst,
            send_sem=halo_send.at[index],
            recv_sem=halo_recv.at[index],
            device_id=target,
            device_id_type=MESH,
        )

    halos = (
        (copy(0, vol_hbm.at[brick_x - 1], plane_ref.at[0], {"bx": me + 1}), has_right, has_left, plane_ref, 0),
        (copy(1, vol_hbm.at[0], plane_ref.at[1], {"bx": me - 1}), has_left, has_right, plane_ref, 1),
        (copy(2, edge_ref.at[0], row_ref.at[0], {"by": col + 1}), has_down, has_up, row_ref, 0),
        (copy(3, edge_ref.at[1], row_ref.at[1], {"by": col - 1}), has_up, has_down, row_ref, 1),
    )
    pl.when(has_up)(halos[3][0].start)
    for halo, sends, receives, ref, slot in halos[:2]:
        pl.when(sends)(halo.start)

    @pl.when(has_down)
    def _():
        pl.semaphore_wait(ready_sem, 1)
        halos[2][0].start()

    for halo, sends, receives, ref, slot in halos:

        @pl.when(jnp.logical_not(receives))
        def _():
            ref[slot] = jnp.zeros(ref.shape[1:], ref.dtype)

    for load in loads[1:]:
        load.wait()

    lane = lax.broadcasted_iota(jnp.int32, (4, 128), 1)
    row_of = jnp.zeros((4, 128), jnp.int32)
    for index in range(tf_ref.shape[0]):
        row_of = jnp.where(lane == index, tf_ref[index], row_of)
    table = jnp.zeros((4, 128), jnp.float32)
    for base in range(0, color_ref.shape[1], 128):
        local = row_of - base
        inside = jnp.logical_and(local >= 0, local < 128)
        found = jnp.take_along_axis(
            color_ref[:, base : base + 128],
            jnp.where(inside, local, 0),
            axis=1,
            mode="promise_in_bounds",
        )
        table = jnp.where(inside, found, table)
    spread = (
        lax.broadcasted_iota(jnp.int32, (half_z, cells_z), 1) // 2
        == lax.broadcasted_iota(jnp.int32, (half_z, cells_z), 0)
    ).astype(jnp.bfloat16)
    rows, fine_rows = half_x * half_y, half_x * brick_y
    repeat = (
        lax.broadcasted_iota(jnp.int32, (fine_rows, rows), 0) // 2
        == lax.broadcasted_iota(jnp.int32, (fine_rows, rows), 1)
    ).astype(jnp.bfloat16)
    coarse = lab_ref[...].reshape(rows, half_z).astype(jnp.float32).astype(jnp.bfloat16)
    wide = jnp.dot(coarse, spread, preferred_element_type=jnp.float32).astype(jnp.bfloat16)
    fine = jnp.dot(repeat, wide, preferred_element_type=jnp.float32).astype(jnp.int32)
    for chan in range(4):
        entries = jnp.broadcast_to(table[chan : chan + 1], (fine_rows, 128))
        values = jnp.take_along_axis(entries, fine, axis=1, mode="promise_in_bounds")
        for x in range(half_x):
            rgbo_ref[x, chan] = values[x * brick_y : (x + 1) * brick_y]

    row = lax.broadcasted_iota(jnp.int32, (brick_y, cells_z), 0)
    depth_lane = lax.broadcasted_iota(jnp.int32, (brick_y, cells_z), 1)

    def dens(x):
        if x < 0:
            return plane_ref[0].astype(jnp.float32)
        if x == brick_x:
            return plane_ref[1].astype(jnp.float32)
        return vol_ref[x].astype(jnp.float32)

    for x in range(brick_x):
        centre = dens(x)
        before = jnp.where(depth_lane == 0, 0.0, pltpu.roll(centre, 1, 1))
        after = jnp.where(depth_lane == cells_z - 1, 0.0, pltpu.roll(centre, cells_z - 1, 1))
        grad_z = (after - before) * 0.5
        grad_sq = grad_z * grad_z
        if 0 < x < brick_x - 1:
            grad_x = (dens(x + 1) - dens(x - 1)) * 0.5
            grad_sq = grad_sq + grad_x * grad_x
        grad_ref[x] = grad_sq
        glow_ref[x] = 1.0 / (1.0 + jnp.exp(-2.0 * centre))

    for halo, sends, receives, ref, slot in halos:
        pl.when(receives)(halo.wait_recv)

    for x in range(brick_x):
        centre = dens(x)
        grad_sq = grad_ref[x]
        if x == 0 or x == brick_x - 1:
            grad_x = (dens(x + 1) - dens(x - 1)) * 0.5
            grad_sq = grad_sq + grad_x * grad_x
        above = jnp.where(row == 0, row_ref[0, x : x + 1, :], pltpu.roll(centre, 1, 0))
        below = jnp.where(
            row == brick_y - 1, row_ref[1, x : x + 1, :], pltpu.roll(centre, brick_y - 1, 0)
        )
        grad_y = (below - above) * 0.5
        grad_sq = grad_sq + grad_y * grad_y
        edge = grad_sq / (1.0 + grad_sq)
        glow = glow_ref[x]
        tau = 6.0 / x_cells * glow * rgbo_ref[x // 2, 3] * (0.25 + edge)
        gain = one_minus_exp(tau) * glow
        for chan in range(3):
            field_ref[x, chan] = gain * rgbo_ref[x // 2, chan]
        field_ref[x, 3] = tau

    shrink = math.gcd(cells_z, 8 * x_cells)
    numer, denom = cells_z // shrink, 8 * x_cells // shrink

    def ahead_of(scaled):
        if denom & (denom - 1) == 0:
            return lax.shift_right_arithmetic(scaled, denom.bit_length() - 1) + cells_z
        return lax.div(scaled + denom * cells_z, denom)

    def composite(view):
        ascending = order_ref[view, 0] == 0
        shear = shear_ref[view]
        color = [jnp.zeros((brick_y, cells_z), jnp.float32) for _ in range(3)]
        depth = jnp.zeros((brick_y, cells_z), jnp.float32)
        for index in range(brick_x):
            x = jnp.where(ascending, index, brick_x - 1 - index)
            ahead = ahead_of(shear * (me * brick_x + x) * numer)
            turn = jnp.where(ahead >= cells_z, ahead - cells_z, ahead)
            source = depth_lane + (cells_z - ahead)
            inside = jnp.logical_and(source >= 0, source < cells_z)
            moved = pltpu.roll(field_ref[x].reshape(4 * brick_y, cells_z), turn, 1)
            seen = jnp.where(inside, jnp.exp(-depth), 0.0)
            for chan in range(3):
                color[chan] = color[chan] + seen * moved[chan * brick_y : (chan + 1) * brick_y]
            depth = depth + jnp.where(inside, moved[3 * brick_y :], 0.0)
        return color + [depth]

    def send_of(view):
        owner = lax.div(view, per_dev)
        local = lax.rem(view, per_dev)
        return pltpu.make_async_remote_copy(
            src_ref=part_ref.at[view],
            dst_ref=got_ref.at[me, local],
            send_sem=part_send.at[view],
            recv_sem=part_recv.at[me, local],
            device_id={"bx": owner},
            device_id_type=MESH,
        )

    def view_at(step):
        turn = lax.div(step, per_dev)
        local = lax.rem(step, per_dev)
        pair, core = lax.div(me, 2), lax.rem(me, 2)
        pair = lax.rem(pair + 1 + lax.div(turn, 2), bricks // 2)
        core = jnp.where(turn == bricks - 2, 1 - core, lax.rem(core + turn, 2))
        return (2 * pair + core) * per_dev + local

    def other_view(step):
        view = view_at(step)
        for chan, values in enumerate(composite(view)):
            part_ref[view, chan] = values
        send_of(view).start()

    if views <= 4:
        for step in range(views - per_dev):
            other_view(jnp.int32(step))
    else:
        pl.loop(0, views - per_dev)(other_view)
    for local in range(per_dev):
        for chan, values in enumerate(composite(me * per_dev + local)):
            got_ref[me, local, chan] = values

    for step in range(1, bricks):
        source = lax.rem(me + step, bricks)
        for local in range(per_dev):
            pltpu.make_async_remote_copy(
                src_ref=part_ref.at[0],
                dst_ref=got_ref.at[source, local],
                send_sem=part_send.at[0],
                recv_sem=part_recv.at[source, local],
                device_id={"bx": source},
                device_id_type=MESH,
            ).wait_recv()

    for local in range(per_dev):
        ascending = order_ref[me * per_dev + local, 0] == 0
        color = [jnp.zeros((brick_y, cells_z), jnp.float32) for _ in range(3)]
        depth = jnp.zeros((brick_y, cells_z), jnp.float32)
        for index in range(bricks):
            brick = jnp.where(ascending, index, bricks - 1 - index)
            seen = jnp.exp(-depth)
            for chan in range(3):
                color[chan] = color[chan] + seen * got_ref[brick, local, chan]
            depth = depth + got_ref[brick, local, 3]
        for chan in range(3):
            out_ref[local, chan] = color[chan]
        out_ref[local, 3] = one_minus_exp(depth)

    for halo, sends, receives, ref, slot in halos:
        pl.when(sends)(halo.wait_send)
    for step in range(views - per_dev):
        send_of(view_at(jnp.int32(step))).wait_send()


def on_device(bricks, columns, volume, labels, depth_order, view_shear, tf_index, color_table):
    brick_x, brick_y, cells_z = volume.shape
    views = depth_order.shape[0]
    per_dev = views // bricks
    image = (4, brick_y, cells_z)
    hbm = pl.BlockSpec(memory_space=pltpu.HBM)
    colors = color_table.T
    arrays = [
        pltpu.with_memory_space_constraint(array, pltpu.HBM)
        for array in (volume, labels, depth_order, view_shear, tf_index, colors)
    ]
    return pl.pallas_call(
        functools.partial(render, bricks, columns),
        out_shape=jax.ShapeDtypeStruct((per_dev,) + image, jnp.float32),
        in_specs=[hbm] * 6,
        out_specs=pl.BlockSpec(memory_space=pltpu.VMEM),
        scratch_shapes=[
            pltpu.VMEM(volume.shape, volume.dtype),
            pltpu.VMEM(labels.shape, labels.dtype),
            pltpu.SMEM(depth_order.shape, depth_order.dtype),
            pltpu.SMEM(view_shear.shape, view_shear.dtype),
            pltpu.SMEM(tf_index.shape, tf_index.dtype),
            pltpu.VMEM(colors.shape, colors.dtype),
            pltpu.VMEM(volume.shape, jnp.float32),
            pltpu.VMEM(volume.shape, jnp.float32),
            pltpu.VMEM((2, brick_y, cells_z), volume.dtype),
            pltpu.VMEM((2, brick_x, cells_z), jnp.float32),
            pltpu.VMEM((2, brick_x, cells_z), jnp.float32),
            pltpu.VMEM((labels.shape[0],) + image, jnp.float32),
            pltpu.VMEM((brick_x,) + image, jnp.float32),
            pltpu.VMEM((views,) + image, jnp.float32),
            pltpu.VMEM((bricks, per_dev) + image, jnp.float32),
            pltpu.SemaphoreType.DMA((4,)),
            pltpu.SemaphoreType.DMA((4,)),
            pltpu.SemaphoreType.DMA((views,)),
            pltpu.SemaphoreType.DMA((bricks, per_dev)),
            pltpu.SemaphoreType.DMA((6,)),
            pltpu.SemaphoreType.REGULAR,
        ],
        compiler_params=pltpu.CompilerParams(
            collective_id=0, has_side_effects=True, vmem_limit_bytes=32 * 2**20
        ),
    )(*arrays)


def solution(mesh):
    return jax.shard_map(
        functools.partial(on_device, mesh.shape["bx"], mesh.shape["by"]),
        mesh=mesh,
        in_specs=(
            P(("grp", "bx"), "by", None),
            P(("grp", "bx"), "by", None),
            P("grp", None),
            P("grp"),
            P(),
            P(),
        ),
        out_specs=P(("grp", "bx"), None, "by", None),
        check_vma=False,
    )
```

```python
import functools
import math

import jax
import jax.numpy as jnp
from jax import lax
from jax.experimental import pallas as pl
from jax.experimental.pallas import tpu as pltpu
from jax.sharding import PartitionSpec as P

MESH = pl.DeviceIdType.MESH


def one_minus_exp(depth):
    series = 1.0 - depth * (1.0 / 6.0)
    for term in (5.0, 4.0, 3.0, 2.0):
        series = 1.0 - depth * (1.0 / term) * series
    return jnp.where(depth < 0.125, depth * series, 1.0 - jnp.exp(-depth))


def render(
    bricks,
    columns,
    vol_hbm,
    lab_hbm,
    order_hbm,
    shear_hbm,
    tf_hbm,
    color_hbm,
    out_ref,
    vol_ref,
    lab_ref,
    order_ref,
    shear_ref,
    tf_ref,
    color_ref,
    glow_ref,
    grad_ref,
    plane_ref,
    edge_ref,
    row_ref,
    rgbo_ref,
    field_ref,
    part_ref,
    got_ref,
    halo_send,
    halo_recv,
    part_send,
    part_recv,
    load_sem,
    ready_sem,
):
    brick_x, brick_y, cells_z = vol_ref.shape
    half_x, half_y, half_z = lab_ref.shape
    views = order_ref.shape[0]
    per_dev = views // bricks
    x_cells = brick_x * bricks
    me = lax.axis_index("bx")
    col = lax.axis_index("by")
    has_left, has_right = me > 0, me < bricks - 1
    has_up, has_down = col > 0, col < columns - 1

    barrier = pltpu.get_barrier_semaphore()
    for step in range(1, bricks):
        other = lax.rem(me + step, bricks)
        pl.semaphore_signal(barrier, inc=1, device_id={"bx": other}, device_id_type=MESH)

    @pl.when(has_down)
    def _():
        pl.semaphore_signal(barrier, inc=1, device_id={"by": col + 1}, device_id_type=MESH)

    pairs = (
        (vol_hbm, vol_ref),
        (lab_hbm, lab_ref),
        (tf_hbm, tf_ref),
        (color_hbm, color_ref),
        (order_hbm, order_ref),
        (shear_hbm, shear_ref),
    )
    loads = [
        pltpu.make_async_copy(source, target, load_sem.at[index])
        for index, (source, target) in enumerate(pairs)
    ]
    for load in loads:
        load.start()
    loads[0].wait()
    for x in range(brick_x):
        plane = vol_ref[x].astype(jnp.float32)
        edge_ref[0, x : x + 1, :] = plane[brick_y - 1 :, :]
        edge_ref[1, x : x + 1, :] = plane[:1, :]

    amount = bricks - 1 + has_up.astype(jnp.int32)
    pl.semaphore_wait(barrier, amount)

    @pl.when(has_up)
    def _():
        pl.semaphore_signal(ready_sem, inc=1, device_id={"by": col - 1}, device_id_type=MESH)

    def copy(index, src, dst, target):
        return pltpu.make_async_remote_copy(
            src_ref=src,
            dst_ref=dst,
            send_sem=halo_send.at[index],
            recv_sem=halo_recv.at[index],
            device_id=target,
            device_id_type=MESH,
        )

    halos = (
        (copy(0, vol_hbm.at[brick_x - 1], plane_ref.at[0], {"bx": me + 1}), has_right, has_left, plane_ref, 0),
        (copy(1, vol_hbm.at[0], plane_ref.at[1], {"bx": me - 1}), has_left, has_right, plane_ref, 1),
        (copy(2, edge_ref.at[0], row_ref.at[0], {"by": col + 1}), has_down, has_up, row_ref, 0),
        (copy(3, edge_ref.at[1], row_ref.at[1], {"by": col - 1}), has_up, has_down, row_ref, 1),
    )
    pl.when(has_up)(halos[3][0].start)
    for halo, sends, receives, ref, slot in halos[:2]:
        pl.when(sends)(halo.start)

    @pl.when(has_down)
    def _():
        pl.semaphore_wait(ready_sem, 1)
        halos[2][0].start()

    for halo, sends, receives, ref, slot in halos:

        @pl.when(jnp.logical_not(receives))
        def _():
            ref[slot] = jnp.zeros(ref.shape[1:], ref.dtype)

    for load in loads[1:]:
        load.wait()

    lane = lax.broadcasted_iota(jnp.int32, (4, 128), 1)
    row_of = jnp.zeros((4, 128), jnp.int32)
    for index in range(tf_ref.shape[0]):
        row_of = jnp.where(lane == index, tf_ref[index], row_of)
    table = jnp.zeros((4, 128), jnp.float32)
    for base in range(0, color_ref.shape[1], 128):
        local = row_of - base
        inside = jnp.logical_and(local >= 0, local < 128)
        found = jnp.take_along_axis(
            color_ref[:, base : base + 128],
            jnp.where(inside, local, 0),
            axis=1,
            mode="promise_in_bounds",
        )
        table = jnp.where(inside, found, table)
    spread = (
        lax.broadcasted_iota(jnp.int32, (half_z, cells_z), 1) // 2
        == lax.broadcasted_iota(jnp.int32, (half_z, cells_z), 0)
    ).astype(jnp.bfloat16)
    rows, fine_rows = half_x * half_y, half_x * brick_y
    repeat = (
        lax.broadcasted_iota(jnp.int32, (fine_rows, rows), 0) // 2
        == lax.broadcasted_iota(jnp.int32, (fine_rows, rows), 1)
    ).astype(jnp.bfloat16)
    coarse = lab_ref[...].reshape(rows, half_z).astype(jnp.float32).astype(jnp.bfloat16)
    wide = jnp.dot(coarse, spread, preferred_element_type=jnp.float32).astype(jnp.bfloat16)
    fine = jnp.dot(repeat, wide, preferred_element_type=jnp.float32).astype(jnp.int32)
    for chan in range(4):
        entries = jnp.broadcast_to(table[chan : chan + 1], (fine_rows, 128))
        values = jnp.take_along_axis(entries, fine, axis=1, mode="promise_in_bounds")
        for x in range(half_x):
            rgbo_ref[x, chan] = values[x * brick_y : (x + 1) * brick_y]

    row = lax.broadcasted_iota(jnp.int32, (brick_y, cells_z), 0)
    depth_lane = lax.broadcasted_iota(jnp.int32, (brick_y, cells_z), 1)

    def dens(x):
        if x < 0:
            return plane_ref[0].astype(jnp.float32)
        if x == brick_x:
            return plane_ref[1].astype(jnp.float32)
        return vol_ref[x].astype(jnp.float32)

    for x in range(brick_x):
        centre = dens(x)
        before = jnp.where(depth_lane == 0, 0.0, pltpu.roll(centre, 1, 1))
        after = jnp.where(depth_lane == cells_z - 1, 0.0, pltpu.roll(centre, cells_z - 1, 1))
        grad_z = (after - before) * 0.5
        grad_sq = grad_z * grad_z
        if 0 < x < brick_x - 1:
            grad_x = (dens(x + 1) - dens(x - 1)) * 0.5
            grad_sq = grad_sq + grad_x * grad_x
        grad_ref[x] = grad_sq
        glow = 1.0 / (1.0 + jnp.exp(-2.0 * centre))
        glow_ref[x] = glow
        field_ref[x, 3] = 6.0 / x_cells * glow * rgbo_ref[x // 2, 3]
        above = jnp.where(row == 0, 0.0, pltpu.roll(centre, 1, 0))
        below = jnp.where(row == brick_y - 1, 0.0, pltpu.roll(centre, brick_y - 1, 0))
        field_ref[x, 0] = below - above

    for halo, sends, receives, ref, slot in halos:
        pl.when(receives)(halo.wait_recv)

    for x in range(brick_x):
        grad_sq = grad_ref[x]
        if x == 0 or x == brick_x - 1:
            grad_x = (dens(x + 1) - dens(x - 1)) * 0.5
            grad_sq = grad_sq + grad_x * grad_x
        above = jnp.where(row == 0, row_ref[0, x : x + 1, :], 0.0)
        below = jnp.where(row == brick_y - 1, row_ref[1, x : x + 1, :], 0.0)
        grad_y = (field_ref[x, 0] + below - above) * 0.5
        grad_sq = grad_sq + grad_y * grad_y
        edge = grad_sq / (1.0 + grad_sq)
        glow = glow_ref[x]
        tau = field_ref[x, 3] * (0.25 + edge)
        gain = one_minus_exp(tau) * glow
        for chan in range(3):
            field_ref[x, chan] = gain * rgbo_ref[x // 2, chan]
        field_ref[x, 3] = tau

    shrink = math.gcd(cells_z, 8 * x_cells)
    numer, denom = cells_z // shrink, 8 * x_cells // shrink

    def ahead_of(scaled):
        if denom & (denom - 1) == 0:
            return lax.shift_right_arithmetic(scaled, denom.bit_length() - 1) + cells_z
        return lax.div(scaled + denom * cells_z, denom)

    def composite(view):
        ascending = order_ref[view, 0] == 0
        shear = shear_ref[view]
        color = [jnp.zeros((brick_y, cells_z), jnp.float32) for _ in range(3)]
        depth = jnp.zeros((brick_y, cells_z), jnp.float32)
        for index in range(brick_x):
            x = jnp.where(ascending, index, brick_x - 1 - index)
            ahead = ahead_of(shear * (me * brick_x + x) * numer)
            turn = jnp.where(ahead >= cells_z, ahead - cells_z, ahead)
            source = depth_lane + (cells_z - ahead)
            inside = jnp.logical_and(source >= 0, source < cells_z)
            moved = pltpu.roll(field_ref[x].reshape(4 * brick_y, cells_z), turn, 1)
            seen = jnp.where(inside, jnp.exp(-depth), 0.0)
            for chan in range(3):
                color[chan] = color[chan] + seen * moved[chan * brick_y : (chan + 1) * brick_y]
            depth = depth + jnp.where(inside, moved[3 * brick_y :], 0.0)
        return color + [depth]

    def send_of(view):
        owner = lax.div(view, per_dev)
        local = lax.rem(view, per_dev)
        return pltpu.make_async_remote_copy(
            src_ref=part_ref.at[view],
            dst_ref=got_ref.at[me, local],
            send_sem=part_send.at[view],
            recv_sem=part_recv.at[me, local],
            device_id={"bx": owner},
            device_id_type=MESH,
        )

    def view_at(step):
        turn = lax.div(step, per_dev)
        local = lax.rem(step, per_dev)
        pair, core = lax.div(me, 2), lax.rem(me, 2)
        pair = lax.rem(pair + 1 + lax.div(turn, 2), bricks // 2)
        core = jnp.where(turn == bricks - 2, 1 - core, lax.rem(core + turn, 2))
        return (2 * pair + core) * per_dev + local

    def other_view(step):
        view = view_at(step)
        for chan, values in enumerate(composite(view)):
            part_ref[view, chan] = values
        send_of(view).start()

    if views <= 4:
        for step in range(views - per_dev):
            other_view(jnp.int32(step))
    else:
        pl.loop(0, views - per_dev)(other_view)
    for local in range(per_dev):
        for chan, values in enumerate(composite(me * per_dev + local)):
            got_ref[me, local, chan] = values

    for step in range(1, bricks):
        source = lax.rem(me + step, bricks)
        for local in range(per_dev):
            pltpu.make_async_remote_copy(
                src_ref=part_ref.at[0],
                dst_ref=got_ref.at[source, local],
                send_sem=part_send.at[0],
                recv_sem=part_recv.at[source, local],
                device_id={"bx": source},
                device_id_type=MESH,
            ).wait_recv()

    for local in range(per_dev):
        ascending = order_ref[me * per_dev + local, 0] == 0
        color = [jnp.zeros((brick_y, cells_z), jnp.float32) for _ in range(3)]
        depth = jnp.zeros((brick_y, cells_z), jnp.float32)
        for index in range(bricks):
            brick = jnp.where(ascending, index, bricks - 1 - index)
            seen = jnp.exp(-depth)
            for chan in range(3):
                color[chan] = color[chan] + seen * got_ref[brick, local, chan]
            depth = depth + got_ref[brick, local, 3]
        for chan in range(3):
            out_ref[local, chan] = color[chan]
        out_ref[local, 3] = one_minus_exp(depth)

    for halo, sends, receives, ref, slot in halos:
        pl.when(sends)(halo.wait_send)
    for step in range(views - per_dev):
        send_of(view_at(jnp.int32(step))).wait_send()


def on_device(bricks, columns, volume, labels, depth_order, view_shear, tf_index, color_table):
    brick_x, brick_y, cells_z = volume.shape
    views = depth_order.shape[0]
    per_dev = views // bricks
    image = (4, brick_y, cells_z)
    hbm = pl.BlockSpec(memory_space=pltpu.HBM)
    colors = color_table.T
    arrays = [
        pltpu.with_memory_space_constraint(array, pltpu.HBM)
        for array in (volume, labels, depth_order, view_shear, tf_index, colors)
    ]
    return pl.pallas_call(
        functools.partial(render, bricks, columns),
        out_shape=jax.ShapeDtypeStruct((per_dev,) + image, jnp.float32),
        in_specs=[hbm] * 6,
        out_specs=pl.BlockSpec(memory_space=pltpu.VMEM),
        scratch_shapes=[
            pltpu.VMEM(volume.shape, volume.dtype),
            pltpu.VMEM(labels.shape, labels.dtype),
            pltpu.SMEM(depth_order.shape, depth_order.dtype),
            pltpu.SMEM(view_shear.shape, view_shear.dtype),
            pltpu.SMEM(tf_index.shape, tf_index.dtype),
            pltpu.VMEM(colors.shape, colors.dtype),
            pltpu.VMEM(volume.shape, jnp.float32),
            pltpu.VMEM(volume.shape, jnp.float32),
            pltpu.VMEM((2, brick_y, cells_z), volume.dtype),
            pltpu.VMEM((2, brick_x, cells_z), jnp.float32),
            pltpu.VMEM((2, brick_x, cells_z), jnp.float32),
            pltpu.VMEM((labels.shape[0],) + image, jnp.float32),
            pltpu.VMEM((brick_x,) + image, jnp.float32),
            pltpu.VMEM((views,) + image, jnp.float32),
            pltpu.VMEM((bricks, per_dev) + image, jnp.float32),
            pltpu.SemaphoreType.DMA((4,)),
            pltpu.SemaphoreType.DMA((4,)),
            pltpu.SemaphoreType.DMA((views,)),
            pltpu.SemaphoreType.DMA((bricks, per_dev)),
            pltpu.SemaphoreType.DMA((6,)),
            pltpu.SemaphoreType.REGULAR,
        ],
        compiler_params=pltpu.CompilerParams(
            collective_id=0, has_side_effects=True, vmem_limit_bytes=32 * 2**20
        ),
    )(*arrays)


def solution(mesh):
    return jax.shard_map(
        functools.partial(on_device, mesh.shape["bx"], mesh.shape["by"]),
        mesh=mesh,
        in_specs=(
            P(("grp", "bx"), "by", None),
            P(("grp", "bx"), "by", None),
            P("grp", None),
            P("grp"),
            P(),
            P(),
        ),
        out_specs=P(("grp", "bx"), None, "by", None),
        check_vma=False,
    )
```
